512 devices in a mesh: col: 32 (over z_lo, x, core), row: 16 (over y, z_hi).
Axes of the slice: x: 4, y: 8, z: 8 (z_hi: 2, z_lo: 4; z = z_hi * 4 + z_lo), core: 2. Of those that a mesh axis runs over, the one named last changes fastest.
Arguments:
- thickness: float32 [4096, 8192], P('row', 'col'), may hold values from -6 to 6
- pairing: int32 [3, 6, 256], replicated, may hold values from 0 to 255, each once within a row
Outputs:
- modes: float32 [4096, 8192], P('row', 'col')
The draws below stay inside these ranges and needn't reach their ends.
All inputs are finite; a program needn't handle non-finite values.
Results may differ from the reference program's by a relative error of at most 0.003.
Values sent between devices are 32-bit elements; how exact they have to be, the bound alone decides.
No kernel may reach another device: no remote copies, remote signals or barrier semaphores. Data moves between devices by JAX's collectives and lax.ppermute only.
A program may use at most 64 MiB of HBM per device.

```python
import jax
import jax.numpy as jnp
from jax import lax

BLK = 128
STEPS = 3
ROUNDS = 6
CELLS = 4096
SNAPS = 8192
N_COL = 32


def steps_of(own_key, shape, cuts, least, top_value):
    def one(position, parts):
        heights = jax.random.uniform(jax.random.fold_in(jax.random.fold_in(own_key, 6), position), (parts,), jnp.float32, least / len(cuts), top_value / len(cuts))
        return jnp.repeat(jnp.exp(heights), shape[position] // parts).reshape((-1,) + (1,) * (len(shape) - position - 1))

    loudness = one(*cuts[0])
    for cut in cuts[1:]:
        loudness = loudness * one(*cut)
    return loudness


def bell_draw(stream_key, dims, width, most, split=(), kind=jnp.bfloat16):
    loudness = steps_of(stream_key, dims, split, -0.22, 0.18) if split else 1.0
    entries = jax.random.normal(stream_key, dims, jnp.float32) * width * loudness
    return jnp.minimum(jnp.maximum(entries, -most), most).astype(kind)


def setup_inputs(seed: int = 0) -> dict:
    key_of = jax.random.split(jax.random.key(seed), 3)
    return {
        "thickness": bell_draw(key_of[0], (CELLS, SNAPS), 1.0, 6.0, ((0, 16), (1, 32)), jnp.float32),
        "pairing": jax.vmap(lambda own: jax.random.permutation(own, 2 * BLK))(jax.random.split(key_of[1], STEPS * ROUNDS)).reshape((STEPS, ROUNDS, 2 * BLK)).astype(jnp.int32),
    }


def jacobi_round(gram_matrix, rotation, ordering):
    half_count = ordering.shape[0] // 2
    leading = ordering[:half_count]
    trailing = ordering[half_count:]
    diagonal = jnp.diagonal(gram_matrix)
    coupling = gram_matrix[leading, trailing]
    angles = 0.5 * jnp.arctan2(2.0 * coupling, diagonal[trailing] - diagonal[leading])
    cosine = jnp.cos(angles)
    sine_part = jnp.sin(angles)
    rotator = jnp.zeros_like(gram_matrix)
    rotator = rotator.at[leading, leading].set(cosine)
    rotator = rotator.at[trailing, trailing].set(cosine)
    rotator = rotator.at[trailing, leading].set(-sine_part)
    rotator = rotator.at[leading, trailing].set(sine_part)
    rows_done = jnp.dot(rotator.T, gram_matrix, precision=lax.Precision.HIGHEST)
    gram_matrix = jnp.dot(rows_done, rotator, precision=lax.Precision.HIGHEST)
    rotation = jnp.dot(rotation, rotator, precision=lax.Precision.HIGHEST)
    return gram_matrix, rotation


def jacobi_solve(gram_matrix, orderings):
    rotation = jnp.eye(gram_matrix.shape[0], dtype=jnp.float32)
    for round_index in range(orderings.shape[0]):
        gram_matrix, rotation = jacobi_round(gram_matrix, rotation, orderings[round_index])
    return gram_matrix, rotation


def reference(thickness, pairing):
    shaped = thickness.reshape(CELLS, N_COL, 2, BLK)
    upper_slots = jnp.transpose(shaped[:, :, 0, :], (1, 0, 2))
    lower_slots = jnp.transpose(shaped[:, :, 1, :], (1, 0, 2))
    floor_value = float(CELLS) ** 0.5
    for section in range(STEPS):
        orderings = pairing[section]

        def solve_pair(blocks):
            pair_block = jnp.concatenate([blocks[0], blocks[1]], axis=1)
            gram_matrix = lax.dot_general(pair_block, pair_block, (((0,), (0,)), ((), ())),
                                          precision=lax.Precision.HIGHEST)
            gram_matrix, rotation = jacobi_solve(gram_matrix, orderings)
            return jnp.dot(pair_block, rotation, precision=lax.Precision.HIGHEST)

        turned = lax.map(solve_pair, (upper_slots, lower_slots))
        if section == STEPS - 1:
            column_total = jnp.sum(turned, axis=1, keepdims=True)
            turned = turned * (column_total / jnp.maximum(jnp.abs(column_total), floor_value))
        new_upper = turned[:, :, :BLK]
        new_lower = turned[:, :, BLK:]
        upper_slots = jnp.concatenate([new_upper[:1], new_lower[:1], new_upper[1:-1]], axis=0)
        lower_slots = jnp.concatenate([new_lower[1:], new_upper[-1:]], axis=0)
    stacked = jnp.stack([upper_slots, lower_slots], axis=2)
    return jnp.transpose(stacked, (1, 0, 2, 3)).reshape(CELLS, SNAPS)
```

```python
import functools
import math

import jax
import jax.numpy as jnp
from jax import lax
from jax.experimental import pallas as pl
from jax.experimental.pallas import tpu as pltpu
from jax.sharding import PartitionSpec as P

F32, BF16 = jnp.float32, jnp.bfloat16
HIGHEST = lax.Precision.HIGHEST


def shifted(array, axis, by):
    peers = lax.axis_size(axis)
    pairs = [(i, i + by) for i in range(peers) if 0 <= i + by < peers]
    return lax.ppermute(array, axis, pairs)


def summed_over_rows(partial):
    peers = lax.axis_size("row")
    rows, width = partial.shape
    parts = partial.reshape(peers, rows // peers, width)
    own = jnp.sum(lax.all_to_all(parts, "row", 0, 0), axis=0)
    spread = jnp.broadcast_to(own[None], (peers,) + own.shape)
    return lax.all_to_all(spread, "row", 0, 0).reshape(rows, width)


def three_parts(x):
    high = x.astype(BF16)
    rest = x - high.astype(F32)
    middle = rest.astype(BF16)
    low = (rest - middle.astype(F32)).astype(BF16)
    return high, middle, low


def columns_by(x, pick):
    dims = (((1,), (0,)), ((), ()))
    high, middle, low = [
        lax.dot_general(part, pick, dims, preferred_element_type=F32) for part in three_parts(x)
    ]
    return high + (middle + low)


def flipped_by(x, pick_t):
    dims = (((1,), (1,)), ((), ()))
    high, middle, low = [
        lax.dot_general(pick_t, part, dims, preferred_element_type=F32) for part in three_parts(x)
    ]
    return high + (middle + low)


def rotation_of(a, b, g):
    x = b - a
    y = 2.0 * g
    top = jnp.maximum(jnp.abs(x), jnp.abs(y))
    none = top == 0.0
    safe = jnp.where(none, 1.0, top)
    xs = x / safe
    ys = y / safe
    inverse = lax.rsqrt(jnp.where(none, 1.0, xs * xs + ys * ys))
    cos2 = jnp.where(none, 1.0, jnp.abs(xs) * inverse)
    sin2 = jnp.abs(ys) * inverse
    h = 0.5 + 0.5 * cos2
    ih = lax.rsqrt(h)
    big = h * ih
    small = 0.5 * sin2 * ih
    c = jnp.where(x >= 0.0, big, small)
    t = jnp.where(x >= 0.0, small, big)
    return c, jnp.where(y < 0.0, -t, t)


def turned(x, c, t):
    half = x.shape[1] // 2
    left, right = x[:, :half], x[:, half:]
    return jnp.concatenate([c * left - t * right, t * left + c * right], axis=1)


def one_hot(column, row):
    return jnp.where(column == row, 1.0, 0.0).astype(BF16)


def solve(gram, rows, columns, want_gram):
    width = gram.shape[0]
    half = width // 2
    rounds = len(rows)
    plain_row = lax.broadcasted_iota(jnp.int32, (1, width), 1)
    plain_column = lax.broadcasted_iota(jnp.int32, (width, 1), 0)
    eye = lax.broadcasted_iota(jnp.int32, (half, half), 0) == lax.broadcasted_iota(
        jnp.int32, (half, half), 1
    )
    rows = [plain_row] + rows + [plain_row]
    columns = [plain_column] + columns + [plain_column]

    def diagonal(block):
        return jnp.sum(jnp.where(eye, block, 0.0), axis=0, keepdims=True)

    gram = columns_by(
        flipped_by(gram, one_hot(columns[1], rows[0])), one_hot(columns[0], rows[1])
    )
    rotation = jnp.where(plain_column == rows[1], 1.0, 0.0).astype(F32)
    for r in range(1, rounds + 1):
        c, t = rotation_of(
            diagonal(gram[:half, :half]), diagonal(gram[half:, half:]), diagonal(gram[:half, half:])
        )
        pick = one_hot(columns[r], rows[r + 1])
        if r < rounds or want_gram:
            pick_t = one_hot(columns[r + 1], rows[r])
            gram = columns_by(turned(flipped_by(turned(gram, c, t), pick_t), c, t), pick)
        rotation = columns_by(turned(rotation, c, t), pick)
    return gram, rotation


def solve_kernel(rounds, gram_ref, rows_ref, columns_ref, rotation_ref):
    rows = [rows_ref[r : r + 1, :] for r in range(rounds)]
    columns = [columns_ref[:, r : r + 1] for r in range(rounds)]
    rotation_ref[...] = solve(gram_ref[...], rows, columns, False)[1]


def jacobi_solve(gram, orderings):
    rounds, width = orderings.shape
    return pl.pallas_call(
        functools.partial(solve_kernel, rounds),
        out_shape=jax.ShapeDtypeStruct((width, width), F32),
    )(gram, orderings, orderings.T)


def shards(thickness, pairing):
    width = thickness.shape[1] // 2
    col_count = lax.axis_size("col")
    peers = lax.axis_size("row")
    position = lax.axis_index("col")
    floor_value = math.sqrt(float(thickness.shape[0] * peers))
    pair_block = thickness
    sections = pairing.shape[0]
    for section in range(sections):
        partial = lax.dot_general(
            pair_block, pair_block, (((0,), (0,)), ((), ())), precision=HIGHEST
        )
        if section == sections - 1:
            totals = jnp.sum(pair_block, axis=0, keepdims=True)
            partial = jnp.concatenate([partial, jnp.pad(totals, ((0, peers - 1), (0, 0)))])
        reduced = summed_over_rows(partial)
        rotation = jacobi_solve(reduced[: 2 * width], pairing[section])
        turned_block = jnp.dot(pair_block, rotation, precision=HIGHEST)
        if section == sections - 1:
            column_total = jnp.dot(
                reduced[2 * width : 2 * width + 1], rotation, precision=HIGHEST
            )
            factor = column_total / jnp.maximum(jnp.abs(column_total), floor_value)
            turned_block = turned_block * factor
        new_upper = turned_block[:, :width]
        new_lower = turned_block[:, width:]
        outgoing = jnp.where(position == 0, new_lower, new_upper)
        arrived = shifted(outgoing, "col", 1)
        returned = shifted(new_lower, "col", -1)
        upper_block = jnp.where(position == 0, new_upper, arrived)
        lower_block = jnp.where(position == col_count - 1, new_upper, returned)
        pair_block = jnp.concatenate([upper_block, lower_block], axis=1)
    return pair_block


def solution(mesh):
    placed = (P("row", "col"), P())
    return jax.shard_map(
        shards, mesh=mesh, in_specs=placed, out_specs=P("row", "col"), check_vma=False
    )
```

```python
import functools
import math

import jax
import jax.numpy as jnp
from jax import lax
from jax.experimental import pallas as pl
from jax.experimental.pallas import tpu as pltpu
from jax.sharding import PartitionSpec as P

F32, BF16 = jnp.float32, jnp.bfloat16
HIGHEST = lax.Precision.HIGHEST


def shifted(array, axis, by):
    peers = lax.axis_size(axis)
    pairs = [(i, i + by) for i in range(peers) if 0 <= i + by < peers]
    return lax.ppermute(array, axis, pairs)


def three_parts(x):
    high = x.astype(BF16)
    rest = x - high.astype(F32)
    middle = rest.astype(BF16)
    low = (rest - middle.astype(F32)).astype(BF16)
    return high, middle, low


def columns_by(x, pick):
    dims = (((1,), (0,)), ((), ()))
    high, middle, low = [
        lax.dot_general(part, pick, dims, preferred_element_type=F32) for part in three_parts(x)
    ]
    return high + (middle + low)


def flipped_by(x, pick_t):
    dims = (((1,), (1,)), ((), ()))
    high, middle, low = [
        lax.dot_general(pick_t, part, dims, preferred_element_type=F32) for part in three_parts(x)
    ]
    return high + (middle + low)


def rotation_of(a, b, g):
    x = b - a
    y = 2.0 * g
    top = jnp.maximum(jnp.abs(x), jnp.abs(y))
    none = top == 0.0
    safe = jnp.where(none, 1.0, top)
    xs = x / safe
    ys = y / safe
    inverse = lax.rsqrt(jnp.where(none, 1.0, xs * xs + ys * ys))
    cos2 = jnp.where(none, 1.0, jnp.abs(xs) * inverse)
    sin2 = jnp.abs(ys) * inverse
    h = 0.5 + 0.5 * cos2
    ih = lax.rsqrt(h)
    big = h * ih
    small = 0.5 * sin2 * ih
    c = jnp.where(x >= 0.0, big, small)
    t = jnp.where(x >= 0.0, small, big)
    return c, jnp.where(y < 0.0, -t, t)


def turned(x, c, t):
    half = x.shape[1] // 2
    left, right = x[:, :half], x[:, half:]
    return jnp.concatenate([c * left - t * right, t * left + c * right], axis=1)


def one_hot(column, row):
    return jnp.where(column == row, 1.0, 0.0).astype(BF16)


def solve(gram, rows, columns, want_gram):
    width = gram.shape[0]
    half = width // 2
    rounds = len(rows)
    plain_row = lax.broadcasted_iota(jnp.int32, (1, width), 1)
    plain_column = lax.broadcasted_iota(jnp.int32, (width, 1), 0)
    eye = lax.broadcasted_iota(jnp.int32, (half, half), 0) == lax.broadcasted_iota(
        jnp.int32, (half, half), 1
    )
    rows = [plain_row] + rows + [plain_row]
    columns = [plain_column] + columns + [plain_column]

    def diagonal(block):
        return jnp.sum(jnp.where(eye, block, 0.0), axis=0, keepdims=True)

    gram = columns_by(
        flipped_by(gram, one_hot(columns[1], rows[0])), one_hot(columns[0], rows[1])
    )
    rotation = jnp.where(plain_column == rows[1], 1.0, 0.0).astype(F32)
    for r in range(1, rounds + 1):
        c, t = rotation_of(
            diagonal(gram[:half, :half]), diagonal(gram[half:, half:]), diagonal(gram[:half, half:])
        )
        pick = one_hot(columns[r], rows[r + 1])
        if r < rounds or want_gram:
            pick_t = one_hot(columns[r + 1], rows[r])
            gram = columns_by(turned(flipped_by(turned(gram, c, t), pick_t), c, t), pick)
        rotation = columns_by(turned(rotation, c, t), pick)
    return gram, rotation


def matmul(x, y):
    return jnp.dot(x, y, precision=HIGHEST, preferred_element_type=F32)


def inner(x, y):
    return lax.dot_general(
        x, y, (((0,), (0,)), ((), ())), precision=HIGHEST, preferred_element_type=F32
    )


def orderings_of(rows_ref, columns_ref):
    rounds = columns_ref.shape[1]
    rows = [rows_ref[r : r + 1, :] for r in range(rounds)]
    columns = [columns_ref[:, r : r + 1] for r in range(rounds)]
    return rows, columns


def square(ref, which=0):
    parts, _, width = ref.shape
    chunk = width // parts
    return ref[:, which * chunk : (which + 1) * chunk, :].reshape(width, width)


def own_gram_kernel(block_ref, out_ref):
    block = block_ref[...]
    width = block.shape[1]
    half = width // 2
    gram = inner(block, block)
    sums = jnp.sum(block, axis=0, keepdims=True)
    spare = jnp.concatenate(
        [sums[:, :half], sums[:, half:], jnp.zeros((half - 2, half), F32)], axis=0
    )
    packed = jnp.concatenate(
        [gram[:half], jnp.concatenate([spare, gram[half:, half:]], axis=1)], axis=0
    )
    out_ref[...] = packed.reshape(out_ref.shape)


def ahead_kernel(
    slots, place_ref, block_ref, before_ref, after_ref, far_before_ref, far_after_ref, out_ref
):
    place = place_ref[0]
    last = slots - 1
    block = block_ref[...]
    before, after = before_ref[...], after_ref[...]
    parts, rows, width = out_ref.shape
    out_ref[:, : rows // 2, :] = inner(
        jnp.where(place == 0, block, before), jnp.where(place == last, block, after)
    ).reshape(parts, rows // 2, width)
    far_before = jnp.where(
        place == 0, after, jnp.where(place == 1, before, far_before_ref[...])
    )
    far_after = jnp.where(
        place == last, before, jnp.where(place == last - 1, after, far_after_ref[...])
    )
    out_ref[:, rows // 2 :, :] = inner(far_before, far_after).reshape(parts, rows // 2, width)


def hand_on_kernel(own_ref, ahead_ref, out_ref):
    parts, rows, width = own_ref.shape
    total = jnp.sum(own_ref[...], axis=0)
    out_ref[:, :rows, :] = jnp.broadcast_to(total[None], (parts, rows, width))
    out_ref[:, rows:, :] = ahead_ref[...]


def spread_kernel(own_rows, in_ref, out_ref):
    out_ref[...] = jnp.broadcast_to(
        jnp.sum(in_ref[:, own_rows:, :], axis=0)[None], out_ref.shape
    )


def post(is_first, blocks, right_ref, left_ref, own_ref):
    at = 0
    for upper, lower in blocks:
        to = at + upper.shape[0]
        own_ref[at:to, :] = upper
        left_ref[at:to, :] = lower
        right_ref[at:to, :] = jnp.where(is_first, lower, upper)
        at = to


def halves(x):
    half = x.shape[1] // 2
    return x[:, :half], x[:, half:]


def gram_halves(gram):
    half = gram.shape[1] // 2
    return gram[:half, :half], gram[half:, half:]


def first_kernel(place_ref, packed_ref, rows_ref, columns_ref, *outs):
    rows, columns = orderings_of(rows_ref, columns_ref)
    packed = square(packed_ref)
    half = packed.shape[1] // 2
    gram = jnp.concatenate(
        [
            packed[:half],
            jnp.concatenate([packed[:half, half:].T, packed[half:, half:]], axis=1),
        ],
        axis=0,
    )
    sums = jnp.concatenate([packed[half : half + 1, :half], packed[half + 1 : half + 2, :half]], 1)
    sums = jnp.broadcast_to(sums, (8, 2 * half))
    gram, rotation = solve(gram, rows, columns, True)
    post(
        place_ref[0] == 0,
        [halves(rotation), gram_halves(gram), halves(matmul(sums, rotation))],
        *outs,
    )


def received(slots, place, arrived_ref, returned_ref, own_ref, sizes):
    pairs = []
    at = 0
    for size in sizes:
        part = slice(at, at + size)
        upper = jnp.where(place == 0, own_ref[part, :], arrived_ref[part, :])
        lower = jnp.where(place == slots - 1, own_ref[part, :], returned_ref[part, :])
        pairs.append((upper, lower))
        at += size
    return pairs


def joined(upper, lower, cross):
    return jnp.concatenate(
        [
            jnp.concatenate([upper, cross], axis=1),
            jnp.concatenate([cross.T, lower], axis=1),
        ],
        axis=0,
    )


def second_kernel(
    slots,
    place_ref,
    arrived_ref,
    returned_ref,
    kept_ref,
    block_ref,
    before_ref,
    after_ref,
    ahead_ref,
    rows_ref,
    columns_ref,
    *outs,
):
    place = place_ref[0]
    rows, columns = orderings_of(rows_ref, columns_ref)
    between = square(ahead_ref)
    depth = between.shape[0]
    half = depth // 2
    (turn_upper, turn_lower), (gram_upper, gram_lower), sums = received(
        slots, place, arrived_ref, returned_ref, kept_ref, (depth, half, 8)
    )
    cross = inner(turn_upper, matmul(between, turn_lower))
    gram, rotation = solve(joined(gram_upper, gram_lower, cross), rows, columns, True)
    before = jnp.where(place == 0, block_ref[...], before_ref[...])
    after = jnp.where(place == slots - 1, block_ref[...], after_ref[...])
    data = jnp.concatenate([matmul(before, turn_upper), matmul(after, turn_lower)], axis=1)
    data = jnp.concatenate([data, jnp.concatenate(sums, axis=1)], axis=0)
    first_turns = matmul(turn_upper, rotation[:half])
    last_turns = matmul(turn_lower, rotation[half:])
    is_first = place == 0
    post(
        is_first,
        [
            halves(first_turns),
            halves(last_turns),
            gram_halves(gram),
            halves(matmul(data, rotation)),
        ],
        *[ref.at[: ref.shape[0] - depth, :] for ref in outs],
    )
    onward = halves(inner(between, first_turns))
    backward = halves(matmul(between, last_turns))
    tail = slice(outs[0].shape[0] - depth, outs[0].shape[0])
    right_ref, left_ref, own_ref = outs
    right_ref[tail, :] = jnp.where(is_first, onward[1], onward[0])
    left_ref[tail, :] = backward[1]
    own_ref[tail, :] = jnp.where(is_first, backward[0], onward[0])


def third_kernel(
    slots,
    floor_value,
    place_ref,
    arrived_ref,
    returned_ref,
    kept_ref,
    ahead_ref,
    packed_ref,
    rows_ref,
    columns_ref,
    right_out_ref,
    left_out_ref,
    own_out_ref,
):
    place = place_ref[0]
    is_first, is_last = place == 0, place == slots - 1
    rows, columns = orderings_of(rows_ref, columns_ref)
    packed = square(packed_ref)
    depth = packed.shape[0]
    half = depth // 2
    cells = right_out_ref.shape[0]
    upper_half = packed[:half]
    raw = jnp.concatenate(
        [
            upper_half,
            jnp.concatenate([upper_half[:, half:].T, packed[half:, half:]], axis=1),
        ],
        axis=0,
    )
    (
        (upper_a, lower_a),
        (upper_b, lower_b),
        (gram_upper, gram_lower),
        data,
        (onward, backward),
    ) = received(
        slots, place, arrived_ref, returned_ref, kept_ref, (depth, depth, half, cells + 8, depth)
    )
    left_a = jnp.where(is_first, upper_b, upper_a)
    left_b = jnp.where(is_first, upper_a, upper_b)
    right_a = jnp.where(is_last, lower_b, lower_a)
    right_b = jnp.where(is_last, lower_a, lower_b)
    cross = (
        inner(onward, right_a)
        + inner(left_a, matmul(square(ahead_ref, 1), right_b))
        + inner(left_b, matmul(raw, right_a) + backward)
    )
    rotation = solve(joined(gram_upper, gram_lower, cross), rows, columns, False)[1]
    data = matmul(jnp.concatenate(data, axis=1), rotation)
    totals = data[cells : cells + 1, :]
    upper, lower = halves(data[:cells, :] * (totals / jnp.maximum(jnp.abs(totals), floor_value)))
    right_out_ref[...] = jnp.where(is_first, lower, upper)
    left_out_ref[...] = lower
    own_out_ref[...] = upper


def whole(array):
    return array, pl.BlockSpec(memory_space=pltpu.VMEM)


def scalar(array):
    return array, pl.BlockSpec(memory_space=pltpu.SMEM)


def call(kernel, outs, microseconds, *operands):
    shapes = [jax.ShapeDtypeStruct(shape, F32) for shape in outs]
    vmem = pl.BlockSpec(memory_space=pltpu.VMEM)
    return pl.pallas_call(
        kernel,
        out_shape=shapes,
        in_specs=[spec for _, spec in operands],
        out_specs=[vmem] * len(shapes),
        compiler_params=pltpu.CompilerParams(vmem_limit_bytes=16 * 2**20),
        cost_estimate=pl.CostEstimate(
            flops=int(microseconds * 1e9), bytes_accessed=2**20, transcendentals=0
        ),
    )(*[array for array, _ in operands])


def shards(thickness, pairing):
    cells, width = thickness.shape
    half = width // 2
    slots = lax.axis_size("col")
    peers = lax.axis_size("row")
    position = lax.axis_index("col")
    place = scalar(jnp.full((1,), position, jnp.int32))
    floor_value = math.sqrt(float(cells * peers))
    orders = [(whole(pairing[s]), whole(pairing[s].T)) for s in range(3)]
    before, after = shifted(thickness, "col", 1), shifted(thickness, "col", -1)
    far_before, far_after = shifted(thickness, "col", 2), shifted(thickness, "col", -2)
    block = whole(thickness)
    chunk = width // peers
    (own,) = call(own_gram_kernel, [(peers, chunk, width)], 30, block)
    own = lax.all_to_all(own, "row", 0, 0)
    (ahead,) = call(
        functools.partial(ahead_kernel, slots),
        [(peers, 2 * chunk, width)],
        2,
        place,
        block,
        whole(before),
        whole(after),
        whole(far_before),
        whole(far_after),
    )
    (handed,) = call(hand_on_kernel, [(peers, 3 * chunk, width)], 1, whole(own), whole(ahead))
    handed = lax.all_to_all(handed, "row", 0, 0)
    (spread,) = call(
        functools.partial(spread_kernel, chunk), [(peers, 2 * chunk, width)], 1, whole(handed)
    )
    ahead = lax.all_to_all(spread, "row", 0, 0)
    packed, ahead = whole(handed), whole(ahead)

    rows = width + half + 8
    right, left, kept = call(
        first_kernel, [(rows, half)] * 3, 6, place, packed, *orders[0]
    )
    arrived, returned = shifted(right, "col", 1), shifted(left, "col", -1)
    rows = 3 * width + half + cells + 8
    right, left, kept = call(
        functools.partial(second_kernel, slots),
        [(rows, half)] * 3,
        8,
        place,
        whole(arrived),
        whole(returned),
        whole(kept),
        block,
        whole(before),
        whole(after),
        ahead,
        *orders[1],
    )
    arrived, returned = shifted(right, "col", 1), shifted(left, "col", -1)
    right, left, kept = call(
        functools.partial(third_kernel, slots, floor_value),
        [(cells, half)] * 3,
        8,
        place,
        whole(arrived),
        whole(returned),
        whole(kept),
        ahead,
        packed,
        *orders[2],
    )
    arrived, returned = shifted(right, "col", 1), shifted(left, "col", -1)
    upper = jnp.where(position == 0, kept, arrived)
    lower = jnp.where(position == slots - 1, kept, returned)
    return jnp.concatenate([upper, lower], axis=1)


def solution(mesh):
    placed = (P("row", "col"), P())
    return jax.shard_map(
        shards, mesh=mesh, in_specs=placed, out_specs=P("row", "col"), check_vma=False
    )
```

```python
import functools
import math

import jax
import jax.numpy as jnp
from jax import lax
from jax.experimental import pallas as pl
from jax.experimental.pallas import tpu as pltpu
from jax.sharding import PartitionSpec as P

F32, BF16 = jnp.float32, jnp.bfloat16
HIGHEST = lax.Precision.HIGHEST


def shifted(array, axis, by):
    peers = lax.axis_size(axis)
    pairs = [(i, i + by) for i in range(peers) if 0 <= i + by < peers]
    return lax.ppermute(array, axis, pairs)


def three_parts(x):
    high = x.astype(BF16)
    rest = x - high.astype(F32)
    middle = rest.astype(BF16)
    low = (rest - middle.astype(F32)).astype(BF16)
    return high, middle, low


def columns_by(x, pick):
    dims = (((1,), (0,)), ((), ()))
    high, middle, low = [
        lax.dot_general(part, pick, dims, preferred_element_type=F32) for part in three_parts(x)
    ]
    return high + (middle + low)


def flipped_by(x, pick_t):
    dims = (((1,), (1,)), ((), ()))
    high, middle, low = [
        lax.dot_general(pick_t, part, dims, preferred_element_type=F32) for part in three_parts(x)
    ]
    return high + (middle + low)


def rotation_of(a, b, g):
    x = b - a
    y = 2.0 * g
    top = jnp.maximum(jnp.abs(x), jnp.abs(y))
    none = top == 0.0
    safe = jnp.where(none, 1.0, top)
    xs = x / safe
    ys = y / safe
    inverse = lax.rsqrt(jnp.where(none, 1.0, xs * xs + ys * ys))
    cos2 = jnp.where(none, 1.0, jnp.abs(xs) * inverse)
    sin2 = jnp.abs(ys) * inverse
    h = 0.5 + 0.5 * cos2
    ih = lax.rsqrt(h)
    big = h * ih
    small = 0.5 * sin2 * ih
    c = jnp.where(x >= 0.0, big, small)
    t = jnp.where(x >= 0.0, small, big)
    return c, jnp.where(y < 0.0, -t, t)


def turned(x, c, t):
    half = x.shape[1] // 2
    left, right = x[:, :half], x[:, half:]
    return jnp.concatenate([c * left - t * right, t * left + c * right], axis=1)


def one_hot(column, row):
    return jnp.where(column == row, 1.0, 0.0).astype(BF16)


def solve(gram, rows, columns, want_gram):
    width = gram.shape[0]
    half = width // 2
    rounds = len(rows)
    plain_row = lax.broadcasted_iota(jnp.int32, (1, width), 1)
    plain_column = lax.broadcasted_iota(jnp.int32, (width, 1), 0)
    eye = lax.broadcasted_iota(jnp.int32, (half, half), 0) == lax.broadcasted_iota(
        jnp.int32, (half, half), 1
    )
    rows = [plain_row] + rows + [plain_row]
    columns = [plain_column] + columns + [plain_column]

    def diagonal(block):
        return jnp.sum(jnp.where(eye, block, 0.0), axis=0, keepdims=True)

    gram = columns_by(
        flipped_by(gram, one_hot(columns[1], rows[0])), one_hot(columns[0], rows[1])
    )
    rotation = jnp.where(plain_column == rows[1], 1.0, 0.0).astype(F32)
    for r in range(1, rounds + 1):
        c, t = rotation_of(
            diagonal(gram[:half, :half]), diagonal(gram[half:, half:]), diagonal(gram[:half, half:])
        )
        pick = one_hot(columns[r], rows[r + 1])
        if r < rounds or want_gram:
            pick_t = one_hot(columns[r + 1], rows[r])
            gram = columns_by(turned(flipped_by(turned(gram, c, t), pick_t), c, t), pick)
        rotation = columns_by(turned(rotation, c, t), pick)
    return gram, rotation


def along_ring(parts):
    rows = lax.axis_size("row")
    rings = [list(range(start, rows, 2)) for start in range(2)]
    return lax.all_to_all(parts, "row", 0, 0, axis_index_groups=rings)


def chip_swap(array):
    slots = lax.axis_size("col")
    return lax.ppermute(array, "col", [(m, m ^ 1) for m in range(slots)])


def outer_swap(array):
    slots = lax.axis_size("col")
    pairs = [(m, min(max(((m + 1) ^ 1) - 1, 0), slots - 1)) for m in range(slots)]
    return lax.ppermute(array, "col", pairs)


def matmul(x, y):
    return jnp.dot(x, y, precision=HIGHEST, preferred_element_type=F32)


def inner(x, y):
    return lax.dot_general(
        x, y, (((0,), (0,)), ((), ())), precision=HIGHEST, preferred_element_type=F32
    )


def orderings_of(rows_ref, columns_ref):
    rounds = columns_ref.shape[1]
    rows = [rows_ref[r : r + 1, :] for r in range(rounds)]
    columns = [columns_ref[:, r : r + 1] for r in range(rounds)]
    return rows, columns


def square(ref, which):
    parts, _, width = ref.shape
    chunk = width // parts
    return ref[:, which * chunk : (which + 1) * chunk, :].reshape(width, width)


def own_gram_kernel(block_ref, out_ref):
    block = block_ref[...]
    width = block.shape[1]
    half = width // 2
    gram = inner(block, block)
    sums = jnp.sum(block, axis=0, keepdims=True)
    spare = jnp.concatenate(
        [sums[:, :half], sums[:, half:], jnp.zeros((half - 2, half), F32)], axis=0
    )
    packed = jnp.concatenate(
        [gram[:half], jnp.concatenate([spare, gram[half:, half:]], axis=1)], axis=0
    )
    out_ref[...] = packed.reshape(out_ref.shape)


def is_even(place_ref):
    return lax.rem(place_ref[0], 2) == 0


def in_order(even, inner_block, outer_block):
    return jnp.where(even, outer_block, inner_block), jnp.where(even, inner_block, outer_block)


def ahead_kernel(
    slots,
    place_ref,
    inner_ref,
    outer_ref,
    far_before_ref,
    far_after_ref,
    out_ref,
    before_ref,
    after_ref,
):
    place = place_ref[0]
    last = slots - 1
    parts, rows, width = out_ref.shape
    chunk = rows // 2
    before, after = in_order(is_even(place_ref), inner_ref[...], outer_ref[...])
    far_before = jnp.where(
        place == 0, after, jnp.where(place == 1, before, far_before_ref[...])
    )
    far_after = jnp.where(
        place == last, before, jnp.where(place == last - 1, after, far_after_ref[...])
    )
    before_ref[...] = far_before
    after_ref[...] = far_after
    out_ref[:, :chunk, :] = inner(before, after).reshape(parts, chunk, width)
    out_ref[:, chunk:, :] = inner(far_before, far_after).reshape(parts, chunk, width)


def total_kernel(in_ref, out_ref):
    out_ref[...] = jnp.sum(in_ref[...], axis=0)


def spread_kernel(one_ref, other_ref, *refs):
    out_ref = refs[-1]
    out_ref[...] = jnp.broadcast_to((one_ref[...] + other_ref[...])[None], out_ref.shape)


def post(place_ref, blocks, inner_out_ref, outer_out_ref):
    upper_inside = is_even(place_ref) & (place_ref[0] != 0)
    at = 0
    for upper, lower in blocks:
        to = at + upper.shape[0]
        inner_out_ref[at:to, :] = jnp.where(upper_inside, upper, lower)
        outer_out_ref[at:to, :] = jnp.where(upper_inside, lower, upper)
        at = to


def halves(x):
    half = x.shape[1] // 2
    return x[:, :half], x[:, half:]


def gram_halves(gram):
    half = gram.shape[1] // 2
    return gram[:half, :half], gram[half:, half:]


def first_kernel(place_ref, sums_ref, rows_ref, columns_ref, *outs):
    rows, columns = orderings_of(rows_ref, columns_ref)
    packed = square(sums_ref, 0)
    half = packed.shape[1] // 2
    gram = jnp.concatenate(
        [
            packed[:half],
            jnp.concatenate([packed[:half, half:].T, packed[half:, half:]], axis=1),
        ],
        axis=0,
    )
    sums = jnp.concatenate([packed[half : half + 1, :half], packed[half + 1 : half + 2, :half]], 1)
    sums = jnp.broadcast_to(sums, (8, 2 * half))
    gram, rotation = solve(gram, rows, columns, True)
    post(
        place_ref,
        [halves(rotation), gram_halves(gram), halves(matmul(sums, rotation))],
        *outs,
    )


def received(even, inner_ref, outer_ref, sizes):
    pairs = []
    at = 0
    for size in sizes:
        part = slice(at, at + size)
        pairs.append(in_order(even, inner_ref[part, :], outer_ref[part, :]))
        at += size
    return pairs


def joined(upper, lower, cross):
    return jnp.concatenate(
        [
            jnp.concatenate([upper, cross], axis=1),
            jnp.concatenate([cross.T, lower], axis=1),
        ],
        axis=0,
    )


def second_kernel(
    slots, place_ref, inner_ref, outer_ref, sums_ref, rows_ref, columns_ref, *outs
):
    place = place_ref[0]
    even = is_even(place_ref)
    rows, columns = orderings_of(rows_ref, columns_ref)
    near = square(sums_ref, 0)
    depth = near.shape[0]
    half = depth // 2
    (turn_upper, turn_lower), (gram_upper, gram_lower), sums = received(
        even, inner_ref, outer_ref, (depth, half, 8)
    )
    onward, backward = inner(near, turn_upper), matmul(near, turn_lower)
    cross = inner(turn_upper, backward)
    first = jnp.concatenate([turn_upper, onward], axis=0)
    last = jnp.concatenate([turn_lower, backward], axis=0)
    gram, rotation = solve(joined(gram_upper, gram_lower, cross), rows, columns, True)
    first, last = matmul(first, rotation[:half]), matmul(last, rotation[half:])
    first_turns, last_turns = first[:depth], last[:depth]
    onward, backward = halves(first[depth:]), halves(last[depth:])
    inner_out_ref, outer_out_ref = outs
    body = inner_out_ref.shape[0] - depth
    post(
        place_ref,
        [
            halves(first_turns),
            halves(last_turns),
            gram_halves(gram),
            halves(matmul(jnp.concatenate(sums, axis=1), rotation)),
        ],
        inner_out_ref.at[:body, :],
        outer_out_ref.at[:body, :],
    )
    is_first = place == 0
    inner_out_ref[body:, :] = jnp.where(
        is_first, onward[1], jnp.where(even, onward[0], backward[1])
    )
    outer_out_ref[body:, :] = jnp.where(
        is_first, backward[0], jnp.where(even, backward[1], onward[0])
    )

    @pl.when(is_first | (place == slots - 1))
    def _():
        outer_out_ref[:depth, :] = last_turns[:, :half]
        outer_out_ref[depth : 2 * depth, :] = first_turns[:, :half]


def third_kernel(
    floor_value,
    place_ref,
    inner_ref,
    outer_ref,
    sums_ref,
    own_ref,
    block_ref,
    before_ref,
    after_ref,
    rows_ref,
    columns_ref,
    inner_out_ref,
    outer_out_ref,
):
    even = is_even(place_ref)
    rows, columns = orderings_of(rows_ref, columns_ref)
    packed = square(own_ref, 0)
    depth = packed.shape[0]
    half = depth // 2
    upper_half = packed[:half]
    raw = jnp.concatenate(
        [
            upper_half,
            jnp.concatenate([upper_half[:, half:].T, packed[half:, half:]], axis=1),
        ],
        axis=0,
    )
    (left_a, right_a), (left_b, right_b), (gram_upper, gram_lower), sums, (onward, backward) = (
        received(even, inner_ref, outer_ref, (depth, depth, half, 8, depth))
    )
    cross = inner(
        jnp.concatenate([onward, left_a, left_b], axis=0),
        jnp.concatenate(
            [right_a, matmul(square(sums_ref, 1), right_b), matmul(raw, right_a) + backward],
            axis=0,
        ),
    )
    block = block_ref[...]
    data = jnp.concatenate(
        [
            matmul(before_ref[...], left_a) + matmul(block, left_b),
            matmul(block, right_a) + matmul(after_ref[...], right_b),
        ],
        axis=1,
    )
    rotation = solve(joined(gram_upper, gram_lower, cross), rows, columns, False)[1]
    data = matmul(data, rotation)
    totals = matmul(jnp.concatenate(sums, axis=1), rotation)[:1]
    data = data * (totals / jnp.maximum(jnp.abs(totals), floor_value))
    post(place_ref, [halves(data)], inner_out_ref, outer_out_ref)


def whole(array):
    return array, pl.BlockSpec(memory_space=pltpu.VMEM)


def after_it(array):
    return array, pl.BlockSpec(memory_space=pl.ANY)


def scalar(array):
    return array, pl.BlockSpec(memory_space=pltpu.SMEM)


def call(kernel, outs, microseconds, *operands):
    shapes = [jax.ShapeDtypeStruct(shape, F32) for shape in outs]
    vmem = pl.BlockSpec(memory_space=pltpu.VMEM)
    return pl.pallas_call(
        kernel,
        out_shape=shapes,
        in_specs=[spec for _, spec in operands],
        out_specs=[vmem] * len(shapes),
        compiler_params=pltpu.CompilerParams(vmem_limit_bytes=10 * 2**20),
        cost_estimate=pl.CostEstimate(
            flops=int(microseconds * 1e9), bytes_accessed=2**20, transcendentals=0
        ),
    )(*[array for array, _ in operands])


def reduced(parts, *first):
    (total,) = call(total_kernel, [parts.shape[1:]], 1, whole(along_ring(parts)))
    across = [(r, r ^ 1) for r in range(lax.axis_size("row"))]
    other = lax.ppermute(total, "row", across)
    (spread,) = call(spread_kernel, [parts.shape], 1, whole(total), whole(other), *first)
    return along_ring(spread)


def shards(thickness, pairing):
    cells, width = thickness.shape
    half = width // 2
    slots = lax.axis_size("col")
    position = lax.axis_index("col")
    place = scalar(jnp.full((1,), position, jnp.int32))
    floor_value = math.sqrt(float(cells * lax.axis_size("row")))
    orders = [(whole(pairing[s]), whole(pairing[s].T)) for s in range(3)]
    block = whole(thickness)
    peers = lax.axis_size("row") // 2
    chunk = width // peers
    inside, outside = chip_swap(thickness), outer_swap(thickness)
    far_before, far_after = shifted(thickness, "col", 2), shifted(thickness, "col", -2)
    (own,) = call(own_gram_kernel, [(peers, chunk, width)], 1, block)
    own = reduced(own)
    ahead, before, after = call(
        functools.partial(ahead_kernel, slots),
        [(peers, 2 * chunk, width), (cells, width), (cells, width)],
        2,
        place,
        whole(inside),
        whole(outside),
        whole(far_before),
        whole(far_after),
    )
    shape = (width + half + 8, half)
    inside, outside = call(first_kernel, [shape] * 2, 6, place, whole(own), *orders[0])
    sums = whole(reduced(ahead, after_it(inside)))
    outside, inside = outer_swap(outside), chip_swap(inside)
    shape = (3 * width + half + 8, half)
    inside, outside = call(
        functools.partial(second_kernel, slots),
        [shape] * 2,
        8,
        place,
        whole(inside),
        whole(outside),
        sums,
        *orders[1],
    )
    outside, inside = outer_swap(outside), chip_swap(inside)
    inside, outside = call(
        functools.partial(third_kernel, floor_value),
        [(cells, half)] * 2,
        8,
        place,
        whole(inside),
        whole(outside),
        sums,
        whole(own),
        block,
        whole(before),
        whole(after),
        *orders[2],
    )
    outside, inside = outer_swap(outside), chip_swap(inside)
    even = lax.rem(position, 2) == 0
    return jnp.concatenate(in_order(even, inside, outside), axis=1)


def solution(mesh):
    placed = (P("row", "col"), P())
    return jax.shard_map(
        shards, mesh=mesh, in_specs=placed, out_specs=P("row", "col"), check_vma=False
    )
```

```python
import functools
import math

import jax
import jax.numpy as jnp
from jax import lax
from jax.experimental import pallas as pl
from jax.experimental.pallas import tpu as pltpu
from jax.sharding import PartitionSpec as P

F32, BF16 = jnp.float32, jnp.bfloat16
HIGHEST = lax.Precision.HIGHEST


def shifted(array, axis, by):
    peers = lax.axis_size(axis)
    pairs = [(i, i + by) for i in range(peers) if 0 <= i + by < peers]
    return lax.ppermute(array, axis, pairs)


def three_parts(x):
    high = x.astype(BF16)
    rest = x - high.astype(F32)
    middle = rest.astype(BF16)
    low = (rest - middle.astype(F32)).astype(BF16)
    return high, middle, low


def columns_by(x, pick):
    dims = (((1,), (0,)), ((), ()))
    high, middle, low = [
        lax.dot_general(part, pick, dims, preferred_element_type=F32) for part in three_parts(x)
    ]
    return high + (middle + low)


def flipped_by(x, pick_t):
    dims = (((1,), (1,)), ((), ()))
    high, middle, low = [
        lax.dot_general(pick_t, part, dims, preferred_element_type=F32) for part in three_parts(x)
    ]
    return high + (middle + low)


def rotation_of(a, b, g):
    x = b - a
    y = 2.0 * g
    top = jnp.maximum(jnp.abs(x), jnp.abs(y))
    none = top == 0.0
    safe = jnp.where(none, 1.0, top)
    xs = x / safe
    ys = y / safe
    inverse = lax.rsqrt(jnp.where(none, 1.0, xs * xs + ys * ys))
    cos2 = jnp.where(none, 1.0, jnp.abs(xs) * inverse)
    sin2 = jnp.abs(ys) * inverse
    h = 0.5 + 0.5 * cos2
    ih = lax.rsqrt(h)
    big = h * ih
    small = 0.5 * sin2 * ih
    c = jnp.where(x >= 0.0, big, small)
    t = jnp.where(x >= 0.0, small, big)
    return c, jnp.where(y < 0.0, -t, t)


def turned(x, c, t):
    half = x.shape[1] // 2
    left, right = x[:, :half], x[:, half:]
    return jnp.concatenate([c * left - t * right, t * left + c * right], axis=1)


def one_hot(column, row):
    return jnp.where(column == row, 1.0, 0.0).astype(BF16)


def solve(gram, rows, columns, want_gram):
    width = gram.shape[0]
    half = width // 2
    rounds = len(rows)
    plain_row = lax.broadcasted_iota(jnp.int32, (1, width), 1)
    plain_column = lax.broadcasted_iota(jnp.int32, (width, 1), 0)
    eye = lax.broadcasted_iota(jnp.int32, (half, half), 0) == lax.broadcasted_iota(
        jnp.int32, (half, half), 1
    )
    rows = [plain_row] + rows + [plain_row]
    columns = [plain_column] + columns + [plain_column]

    def diagonal(block):
        return jnp.sum(jnp.where(eye, block, 0.0), axis=0, keepdims=True)

    gram = columns_by(
        flipped_by(gram, one_hot(columns[1], rows[0])), one_hot(columns[0], rows[1])
    )
    rotation = jnp.where(plain_column == rows[1], 1.0, 0.0).astype(F32)
    for r in range(1, rounds + 1):
        c, t = rotation_of(
            diagonal(gram[:half, :half]), diagonal(gram[half:, half:]), diagonal(gram[:half, half:])
        )
        pick = one_hot(columns[r], rows[r + 1])
        if r < rounds or want_gram:
            pick_t = one_hot(columns[r + 1], rows[r])
            gram = columns_by(turned(flipped_by(turned(gram, c, t), pick_t), c, t), pick)
        rotation = columns_by(turned(rotation, c, t), pick)
    return gram, rotation


def along_ring(parts):
    rows = lax.axis_size("row")
    rings = [list(range(start, rows, 2)) for start in range(2)]
    return lax.all_to_all(parts, "row", 0, 0, axis_index_groups=rings)


def chip_swap(array):
    slots = lax.axis_size("col")
    return lax.ppermute(array, "col", [(m, m ^ 1) for m in range(slots)])


def outer_swap(array):
    slots = lax.axis_size("col")
    pairs = [(m, min(max(((m + 1) ^ 1) - 1, 0), slots - 1)) for m in range(slots)]
    return lax.ppermute(array, "col", pairs)


def matmul(x, y):
    return jnp.dot(x, y, precision=HIGHEST, preferred_element_type=F32)


def inner(x, y):
    return lax.dot_general(
        x, y, (((0,), (0,)), ((), ())), precision=HIGHEST, preferred_element_type=F32
    )


def orderings_of(rows_ref, columns_ref):
    rounds = columns_ref.shape[1]
    rows = [rows_ref[r : r + 1, :] for r in range(rounds)]
    columns = [columns_ref[:, r : r + 1] for r in range(rounds)]
    return rows, columns


def square(ref, which):
    parts, _, width = ref.shape
    chunk = width // parts
    return ref[:, which * chunk : (which + 1) * chunk, :].reshape(width, width)


def own_gram_kernel(block_ref, out_ref):
    block = block_ref[...]
    width = block.shape[1]
    half = width // 2
    gram = inner(block, block)
    sums = jnp.sum(block, axis=0, keepdims=True)
    spare = jnp.concatenate(
        [sums[:, :half], sums[:, half:], jnp.zeros((half - 2, half), F32)], axis=0
    )
    packed = jnp.concatenate(
        [gram[:half], jnp.concatenate([spare, gram[half:, half:]], axis=1)], axis=0
    )
    out_ref[...] = packed.reshape(out_ref.shape)


def is_even(place_ref):
    return lax.rem(place_ref[0], 2) == 0


def in_order(even, inner_block, outer_block):
    return jnp.where(even, outer_block, inner_block), jnp.where(even, inner_block, outer_block)


def ahead_kernel(
    slots,
    place_ref,
    outer_ref,
    inner_ref,
    far_after_ref,
    far_before_ref,
    out_ref,
    before_ref,
    after_ref,
):
    place = place_ref[0]
    last = slots - 1
    parts, rows, width = out_ref.shape
    chunk = rows // 2
    before, after = in_order(is_even(place_ref), inner_ref[...], outer_ref[...])
    far_before = jnp.where(
        place == 0, after, jnp.where(place == 1, before, far_before_ref[...])
    )
    far_after = jnp.where(
        place == last, before, jnp.where(place == last - 1, after, far_after_ref[...])
    )
    before_ref[...] = far_before
    after_ref[...] = far_after
    out_ref[:, :chunk, :] = inner(before, after).reshape(parts, chunk, width)
    out_ref[:, chunk:, :] = inner(far_before, far_after).reshape(parts, chunk, width)


def total_kernel(in_ref, out_ref):
    out_ref[...] = jnp.sum(in_ref[...], axis=0)


def spread_kernel(one_ref, other_ref, *refs):
    out_ref = refs[-1]
    out_ref[...] = jnp.broadcast_to((one_ref[...] + other_ref[...])[None], out_ref.shape)


def post(place_ref, blocks, inner_out_ref, outer_out_ref):
    upper_inside = is_even(place_ref) & (place_ref[0] != 0)
    at = 0
    for upper, lower in blocks:
        to = at + upper.shape[0]
        inner_out_ref[at:to, :] = jnp.where(upper_inside, upper, lower)
        outer_out_ref[at:to, :] = jnp.where(upper_inside, lower, upper)
        at = to


def halves(x):
    half = x.shape[1] // 2
    return x[:, :half], x[:, half:]


def gram_halves(gram):
    half = gram.shape[1] // 2
    return gram[:half, :half], gram[half:, half:]


def first_kernel(
    place_ref, sums_ref, block_ref, rows_ref, columns_ref, inner_out_ref, outer_out_ref, data_ref, pair_ref
):
    rows, columns = orderings_of(rows_ref, columns_ref)
    packed = square(sums_ref, 0)
    half = packed.shape[1] // 2
    gram = jnp.concatenate(
        [
            packed[:half],
            jnp.concatenate([packed[:half, half:].T, packed[half:, half:]], axis=1),
        ],
        axis=0,
    )
    sums = jnp.concatenate([packed[half : half + 1, :half], packed[half + 1 : half + 2, :half]], 1)
    sums = jnp.broadcast_to(sums, (8, 2 * half))
    gram, rotation = solve(gram, rows, columns, True)
    upper, lower = halves(rotation)
    post(
        place_ref,
        [(upper, lower), (lower, upper), gram_halves(gram), halves(matmul(sums, rotation))],
        inner_out_ref,
        outer_out_ref,
    )
    is_first = place_ref[0] == 0
    data = matmul(block_ref[...], rotation)
    data_ref[:, :half] = jnp.where(is_first, data[:, half:], data[:, :half])
    data_ref[:, half:] = jnp.where(is_first, data[:, :half], data[:, half:])
    pair_ref[...] = jnp.where(is_first, gram[:half, half:], gram[half:, :half])


def received(even, inner_ref, outer_ref, sizes):
    pairs = []
    at = 0
    for size in sizes:
        part = slice(at, at + size)
        pairs.append(in_order(even, inner_ref[part, :], outer_ref[part, :]))
        at += size
    return pairs


def joined(upper, lower, cross):
    return jnp.concatenate(
        [
            jnp.concatenate([upper, cross], axis=1),
            jnp.concatenate([cross.T, lower], axis=1),
        ],
        axis=0,
    )


def second_kernel(
    place_ref, inner_ref, outer_ref, sums_ref, rows_ref, columns_ref, *outs
):
    even = is_even(place_ref)
    rows, columns = orderings_of(rows_ref, columns_ref)
    near = square(sums_ref, 0)
    depth = near.shape[0]
    half = depth // 2
    (turn_upper, turn_lower), (other_upper, other_lower), (gram_upper, gram_lower), sums = (
        received(even, inner_ref, outer_ref, (depth, depth, half, 8))
    )
    backward = matmul(near, turn_lower)
    cross = inner(turn_upper, backward)
    onward = jnp.concatenate(
        [turn_upper, inner(matmul(near, other_lower), turn_upper)], axis=0
    )
    backward = jnp.concatenate([turn_lower, inner(other_upper, backward)], axis=0)
    gram, rotation = solve(joined(gram_upper, gram_lower, cross), rows, columns, True)
    onward, backward = matmul(onward, rotation[:half]), matmul(backward, rotation[half:])
    onward = jnp.concatenate([onward, rotation[half:]], axis=0)
    backward = jnp.concatenate([backward, rotation[:half]], axis=0)
    inner_out_ref, outer_out_ref = outs
    body = 2 * depth
    post(
        place_ref,
        [gram_halves(gram), halves(matmul(jnp.concatenate(sums, axis=1), rotation))],
        inner_out_ref.at[body:, :],
        outer_out_ref.at[body:, :],
    )
    is_first = place_ref[0] == 0
    onward, backward = halves(onward), halves(backward)
    inner_out_ref[:body, :] = jnp.where(
        is_first, onward[1], jnp.where(even, onward[0], backward[1])
    )
    outer_out_ref[:body, :] = jnp.where(
        is_first, backward[0], jnp.where(even, backward[1], onward[0])
    )


def third_kernel(
    floor_value,
    place_ref,
    outer_ref,
    inner_ref,
    sums_ref,
    data_ref,
    pair_ref,
    before_ref,
    after_ref,
    rows_ref,
    columns_ref,
    inner_out_ref,
    outer_out_ref,
):
    even = is_even(place_ref)
    rows, columns = orderings_of(rows_ref, columns_ref)
    half = pair_ref.shape[0]
    (
        (left_far, right_far),
        (onward, backward),
        (left_near, right_near),
        (gram_upper, gram_lower),
        sums,
    ) = received(even, inner_ref, outer_ref, (2 * half, half, half, half, 8))
    cross = inner(
        jnp.concatenate([onward, left_far, left_near], axis=0),
        jnp.concatenate(
            [
                right_near,
                matmul(square(sums_ref, 1), right_far),
                matmul(pair_ref[...], right_near) + backward,
            ],
            axis=0,
        ),
    )
    data = jnp.concatenate(
        [
            matmul(before_ref[...], left_far) + matmul(data_ref[:, half:], left_near),
            matmul(data_ref[:, :half], right_near) + matmul(after_ref[...], right_far),
        ],
        axis=1,
    )
    rotation = solve(joined(gram_upper, gram_lower, cross), rows, columns, False)[1]
    data = matmul(data, rotation)
    totals = matmul(jnp.concatenate(sums, axis=1), rotation)[:1]
    data = data * (totals / jnp.maximum(jnp.abs(totals), floor_value))
    post(place_ref, [halves(data)], inner_out_ref, outer_out_ref)


def whole(array):
    return array, pl.BlockSpec(memory_space=pltpu.VMEM)


def after_it(array):
    return array, pl.BlockSpec(memory_space=pl.ANY)


def scalar(array):
    return array, pl.BlockSpec(memory_space=pltpu.SMEM)


def call(kernel, outs, microseconds, *operands):
    shapes = [jax.ShapeDtypeStruct(shape, F32) for shape in outs]
    vmem = pl.BlockSpec(memory_space=pltpu.VMEM)
    return pl.pallas_call(
        kernel,
        out_shape=shapes,
        in_specs=[spec for _, spec in operands],
        out_specs=[vmem] * len(shapes),
        compiler_params=pltpu.CompilerParams(vmem_limit_bytes=10 * 2**20),
        cost_estimate=pl.CostEstimate(
            flops=int(microseconds * 1e9), bytes_accessed=2**20, transcendentals=0
        ),
    )(*[array for array, _ in operands])


def reduced(parts, *first):
    (total,) = call(total_kernel, [parts.shape[1:]], 1, whole(along_ring(parts)))
    across = [(r, r ^ 1) for r in range(lax.axis_size("row"))]
    other = lax.ppermute(total, "row", across)
    (spread,) = call(spread_kernel, [parts.shape], 1, whole(total), whole(other), *first)
    return along_ring(spread)


def shards(thickness, pairing):
    cells, width = thickness.shape
    half = width // 2
    slots = lax.axis_size("col")
    position = lax.axis_index("col")
    place = scalar(jnp.full((1,), position, jnp.int32))
    floor_value = math.sqrt(float(cells * lax.axis_size("row")))
    orders = [(whole(pairing[s]), whole(pairing[s].T)) for s in range(3)]
    block = whole(thickness)
    peers = lax.axis_size("row") // 2
    chunk = width // peers
    inside, outside = chip_swap(thickness), outer_swap(thickness)
    far_before, far_after = shifted(thickness, "col", 2), shifted(thickness, "col", -2)
    (own,) = call(own_gram_kernel, [(peers, chunk, width)], 1, block)
    own = reduced(own)
    ahead, before, after = call(
        functools.partial(ahead_kernel, slots),
        [(peers, 2 * chunk, width), (cells, width), (cells, width)],
        2,
        place,
        whole(outside),
        whole(inside),
        whole(far_after),
        whole(far_before),
    )
    shape = (2 * width + half + 8, half)
    inside, outside, data, pair = call(
        first_kernel,
        [shape, shape, (cells, width), (half, half)],
        6,
        place,
        whole(own),
        block,
        *orders[0],
    )
    sums = whole(reduced(ahead, after_it(inside)))
    outside, inside = outer_swap(outside), chip_swap(inside)
    inside, outside = call(
        second_kernel,
        [shape] * 2,
        8,
        place,
        whole(inside),
        whole(outside),
        sums,
        *orders[1],
    )
    outside, inside = outer_swap(outside), chip_swap(inside)
    inside, outside = call(
        functools.partial(third_kernel, floor_value),
        [(cells, half)] * 2,
        8,
        place,
        whole(outside),
        whole(inside),
        sums,
        whole(data),
        whole(pair),
        whole(before),
        whole(after),
        *orders[2],
    )
    outside, inside = outer_swap(outside), chip_swap(inside)
    even = lax.rem(position, 2) == 0
    return jnp.concatenate(in_order(even, inside, outside), axis=1)


def solution(mesh):
    placed = (P("row", "col"), P())
    return jax.shard_map(
        shards, mesh=mesh, in_specs=placed, out_specs=P("row", "col"), check_vma=False
    )
```

```python
import functools
import math

import jax
import jax.numpy as jnp
from jax import lax
from jax.experimental import pallas as pl
from jax.experimental.pallas import tpu as pltpu
from jax.sharding import PartitionSpec as P

F32, BF16 = jnp.float32, jnp.bfloat16
HIGHEST = lax.Precision.HIGHEST


def shifted(array, axis, by):
    peers = lax.axis_size(axis)
    pairs = [(i, i + by) for i in range(peers) if 0 <= i + by < peers]
    return lax.ppermute(array, axis, pairs)


def three_parts(x):
    high = x.astype(BF16)
    rest = x - high.astype(F32)
    middle = rest.astype(BF16)
    low = (rest - middle.astype(F32)).astype(BF16)
    return high, middle, low


def columns_by(x, pick):
    dims = (((1,), (0,)), ((), ()))
    high, middle, low = [
        lax.dot_general(part, pick, dims, preferred_element_type=F32) for part in three_parts(x)
    ]
    return high + (middle + low)


def two_parts(x):
    return three_parts(x)[:2]


def off_diagonal_by(x, diagonal, pick):
    rows, few = x.shape[0], diagonal.shape[0]
    dims = (((1,), (0,)), ((), ()))
    stacked = jnp.concatenate(two_parts(x) + three_parts(diagonal), axis=0)
    moved = lax.dot_general(stacked, pick, dims, preferred_element_type=F32)
    high, middle, low = [moved[2 * rows + i * few : 2 * rows + (i + 1) * few] for i in range(3)]
    return moved[:rows] + moved[rows : 2 * rows], high + (middle + low)


def flipped_by(x, pick_t):
    dims = (((1,), (1,)), ((), ()))
    high, middle = [
        lax.dot_general(pick_t, part, dims, preferred_element_type=F32) for part in two_parts(x)
    ]
    return high + middle


def rotation_of(a, b, g):
    x = b - a
    y = 2.0 * g
    top = jnp.maximum(jnp.abs(x), jnp.abs(y))
    none = top == 0.0
    safe = jnp.where(none, 1.0, top)
    xs = x / safe
    ys = y / safe
    inverse = lax.rsqrt(jnp.where(none, 1.0, xs * xs + ys * ys))
    cos2 = jnp.where(none, 1.0, jnp.abs(xs) * inverse)
    sin2 = jnp.abs(ys) * inverse
    h = 0.5 + 0.5 * cos2
    ih = lax.rsqrt(h)
    big = h * ih
    small = 0.5 * sin2 * ih
    c = jnp.where(x >= 0.0, big, small)
    t = jnp.where(x >= 0.0, small, big)
    return c, jnp.where(y < 0.0, -t, t)


def turned(x, c, t):
    half = x.shape[1] // 2
    left, right = x[:, :half], x[:, half:]
    return jnp.concatenate([c * left - t * right, t * left + c * right], axis=1)


def one_hot(column, row):
    return jnp.where(column == row, 1.0, 0.0).astype(BF16)


def solve(gram, rows, columns, want_gram):
    width = gram.shape[0]
    half = width // 2
    rounds = len(rows)
    plain_row = lax.broadcasted_iota(jnp.int32, (1, width), 1)
    plain_column = lax.broadcasted_iota(jnp.int32, (width, 1), 0)
    on_diagonal = plain_row == plain_column
    eye = on_diagonal[:half, :half]
    rows = [plain_row] + rows + [plain_row]
    columns = [plain_column] + columns + [plain_column]

    diagonal = jnp.sum(jnp.where(on_diagonal, gram, 0.0), axis=0, keepdims=True)
    gram = flipped_by(jnp.where(on_diagonal, 0.0, gram), one_hot(columns[1], rows[0]))
    gram, diagonal = off_diagonal_by(
        gram, jnp.broadcast_to(diagonal, (16, width)), one_hot(columns[0], rows[1])
    )
    rotation = jnp.where(plain_column == rows[1], 1.0, 0.0).astype(F32)
    for r in range(1, rounds + 1):
        a, b = diagonal[:1, :half], diagonal[:1, half:]
        g = jnp.sum(jnp.where(eye, gram[:half, half:], 0.0), axis=0, keepdims=True)
        c, t = rotation_of(a, b, g)
        pick = one_hot(columns[r], rows[r + 1])
        if r < rounds or want_gram:
            pick_t = one_hot(columns[r + 1], rows[r])
            partners = jnp.concatenate([rows[r][:, half:], rows[r][:, :half]], axis=1)
            settled = (columns[r + 1] == rows[r]) | (columns[r + 1] == partners)
            gram = turned(flipped_by(turned(gram, c, t), pick_t), c, t)
            moved = t * (t * (b - a) - 2.0 * (c * g))
            diagonal = jnp.broadcast_to(
                jnp.concatenate([a + moved, b - moved], axis=1), (16, width)
            )
            gram, diagonal = off_diagonal_by(jnp.where(settled, 0.0, gram), diagonal, pick)
        rotation = columns_by(turned(rotation, c, t), pick)
    return jnp.where(on_diagonal, diagonal[:1], gram), rotation


def along_ring(parts):
    rows = lax.axis_size("row")
    rings = [list(range(start, rows, 2)) for start in range(2)]
    return lax.all_to_all(parts, "row", 0, 0, axis_index_groups=rings)


def chip_swap(array):
    slots = lax.axis_size("col")
    return lax.ppermute(array, "col", [(m, m ^ 1) for m in range(slots)])


def outer_swap(array):
    slots = lax.axis_size("col")
    pairs = [(m, min(max(((m + 1) ^ 1) - 1, 0), slots - 1)) for m in range(slots)]
    return lax.ppermute(array, "col", pairs)


def matmul(x, y):
    return jnp.dot(x, y, precision=HIGHEST, preferred_element_type=F32)


def inner(x, y):
    return lax.dot_general(
        x, y, (((0,), (0,)), ((), ())), precision=HIGHEST, preferred_element_type=F32
    )


def orderings_of(rows_ref, columns_ref):
    rounds = columns_ref.shape[1]
    rows = [rows_ref[r : r + 1, :] for r in range(rounds)]
    columns = [columns_ref[:, r : r + 1] for r in range(rounds)]
    return rows, columns


def square(ref, which):
    parts, _, width = ref.shape
    chunk = width // parts
    return ref[:, which * chunk : (which + 1) * chunk, :].reshape(width, width)


def own_gram_kernel(block_ref, out_ref):
    block = block_ref[...]
    width = block.shape[1]
    half = width // 2
    gram = inner(block, block)
    sums = jnp.sum(block, axis=0, keepdims=True)
    spare = jnp.concatenate(
        [sums[:, :half], sums[:, half:], jnp.zeros((half - 2, half), F32)], axis=0
    )
    packed = jnp.concatenate(
        [gram[:half], jnp.concatenate([spare, gram[half:, half:]], axis=1)], axis=0
    )
    out_ref[...] = packed.reshape(out_ref.shape)


def is_even(place_ref):
    return lax.rem(place_ref[0], 2) == 0


def in_order(even, inner_block, outer_block):
    return jnp.where(even, outer_block, inner_block), jnp.where(even, inner_block, outer_block)


def ahead_kernel(
    slots,
    place_ref,
    outer_ref,
    inner_ref,
    far_after_ref,
    far_before_ref,
    out_ref,
    before_ref,
    after_ref,
):
    place = place_ref[0]
    last = slots - 1
    parts, rows, width = out_ref.shape
    chunk = rows // 2
    before, after = in_order(is_even(place_ref), inner_ref[...], outer_ref[...])
    far_before = jnp.where(
        place == 0, after, jnp.where(place == 1, before, far_before_ref[...])
    )
    far_after = jnp.where(
        place == last, before, jnp.where(place == last - 1, after, far_after_ref[...])
    )
    before_ref[...] = far_before
    after_ref[...] = far_after
    out_ref[:, :chunk, :] = inner(before, after).reshape(parts, chunk, width)
    out_ref[:, chunk:, :] = inner(far_before, far_after).reshape(parts, chunk, width)


def total_kernel(in_ref, out_ref):
    out_ref[...] = jnp.sum(in_ref[...], axis=0)


def spread_kernel(one_ref, other_ref, *refs):
    out_ref = refs[-1]
    out_ref[...] = jnp.broadcast_to((one_ref[...] + other_ref[...])[None], out_ref.shape)


def post(place_ref, blocks, inner_out_ref, outer_out_ref):
    upper_inside = is_even(place_ref) & (place_ref[0] != 0)
    at = 0
    for upper, lower in blocks:
        to = at + upper.shape[0]
        inner_out_ref[at:to, :] = jnp.where(upper_inside, upper, lower)
        outer_out_ref[at:to, :] = jnp.where(upper_inside, lower, upper)
        at = to


def halves(x):
    half = x.shape[1] // 2
    return x[:, :half], x[:, half:]


def gram_halves(gram):
    half = gram.shape[1] // 2
    return gram[:half, :half], gram[half:, half:]


def first_kernel(
    place_ref, sums_ref, block_ref, rows_ref, columns_ref, inner_out_ref, outer_out_ref, data_ref, pair_ref
):
    rows, columns = orderings_of(rows_ref, columns_ref)
    packed = square(sums_ref, 0)
    half = packed.shape[1] // 2
    gram = jnp.concatenate(
        [
            packed[:half],
            jnp.concatenate([packed[:half, half:].T, packed[half:, half:]], axis=1),
        ],
        axis=0,
    )
    sums = jnp.concatenate([packed[half : half + 1, :half], packed[half + 1 : half + 2, :half]], 1)
    sums = jnp.broadcast_to(sums, (8, 2 * half))
    gram, rotation = solve(gram, rows, columns, True)
    upper, lower = halves(rotation)
    post(
        place_ref,
        [(upper, lower), (lower, upper), gram_halves(gram), halves(matmul(sums, rotation))],
        inner_out_ref,
        outer_out_ref,
    )
    is_first = place_ref[0] == 0
    data = matmul(block_ref[...], rotation)
    data_ref[:, :half] = jnp.where(is_first, data[:, half:], data[:, :half])
    data_ref[:, half:] = jnp.where(is_first, data[:, :half], data[:, half:])
    pair_ref[...] = jnp.where(is_first, gram[:half, half:], gram[half:, :half])


def received(even, inner_ref, outer_ref, sizes):
    pairs = []
    at = 0
    for size in sizes:
        part = slice(at, at + size)
        pairs.append(in_order(even, inner_ref[part, :], outer_ref[part, :]))
        at += size
    return pairs


def joined(upper, lower, cross):
    return jnp.concatenate(
        [
            jnp.concatenate([upper, cross], axis=1),
            jnp.concatenate([cross.T, lower], axis=1),
        ],
        axis=0,
    )


def second_kernel(
    place_ref, inner_ref, outer_ref, sums_ref, rows_ref, columns_ref, *outs
):
    even = is_even(place_ref)
    rows, columns = orderings_of(rows_ref, columns_ref)
    near = square(sums_ref, 0)
    depth = near.shape[0]
    half = depth // 2
    (turn_upper, turn_lower), (other_upper, other_lower), (gram_upper, gram_lower), sums = (
        received(even, inner_ref, outer_ref, (depth, depth, half, 8))
    )
    backward = matmul(near, turn_lower)
    cross = inner(turn_upper, backward)
    onward = jnp.concatenate(
        [turn_upper, inner(matmul(near, other_lower), turn_upper)], axis=0
    )
    backward = jnp.concatenate([turn_lower, inner(other_upper, backward)], axis=0)
    gram, rotation = solve(joined(gram_upper, gram_lower, cross), rows, columns, True)
    onward, backward = matmul(onward, rotation[:half]), matmul(backward, rotation[half:])
    onward = jnp.concatenate([onward, rotation[half:]], axis=0)
    backward = jnp.concatenate([backward, rotation[:half]], axis=0)
    inner_out_ref, outer_out_ref = outs
    body = 2 * depth
    post(
        place_ref,
        [gram_halves(gram), halves(matmul(jnp.concatenate(sums, axis=1), rotation))],
        inner_out_ref.at[body:, :],
        outer_out_ref.at[body:, :],
    )
    is_first = place_ref[0] == 0
    onward, backward = halves(onward), halves(backward)
    inner_out_ref[:body, :] = jnp.where(
        is_first, onward[1], jnp.where(even, onward[0], backward[1])
    )
    outer_out_ref[:body, :] = jnp.where(
        is_first, backward[0], jnp.where(even, backward[1], onward[0])
    )


def third_kernel(
    floor_value,
    place_ref,
    outer_ref,
    inner_ref,
    sums_ref,
    data_ref,
    pair_ref,
    before_ref,
    after_ref,
    rows_ref,
    columns_ref,
    inner_out_ref,
    outer_out_ref,
):
    even = is_even(place_ref)
    rows, columns = orderings_of(rows_ref, columns_ref)
    half = pair_ref.shape[0]
    (
        (left_far, right_far),
        (onward, backward),
        (left_near, right_near),
        (gram_upper, gram_lower),
        sums,
    ) = received(even, inner_ref, outer_ref, (2 * half, half, half, half, 8))
    cross = inner(
        jnp.concatenate([onward, left_far, left_near], axis=0),
        jnp.concatenate(
            [
                right_near,
                matmul(square(sums_ref, 1), right_far),
                matmul(pair_ref[...], right_near) + backward,
            ],
            axis=0,
        ),
    )
    data = jnp.concatenate(
        [
            matmul(before_ref[...], left_far) + matmul(data_ref[:, half:], left_near),
            matmul(data_ref[:, :half], right_near) + matmul(after_ref[...], right_far),
        ],
        axis=1,
    )
    rotation = solve(joined(gram_upper, gram_lower, cross), rows, columns, False)[1]
    data = matmul(data, rotation)
    totals = matmul(jnp.concatenate(sums, axis=1), rotation)[:1]
    data = data * (totals / jnp.maximum(jnp.abs(totals), floor_value))
    post(place_ref, [halves(data)], inner_out_ref, outer_out_ref)


def whole(array):
    return array, pl.BlockSpec(memory_space=pltpu.VMEM)


def after_it(array):
    return array, pl.BlockSpec(memory_space=pl.ANY)


def scalar(array):
    return array, pl.BlockSpec(memory_space=pltpu.SMEM)


def call(kernel, outs, microseconds, *operands):
    shapes = [jax.ShapeDtypeStruct(shape, F32) for shape in outs]
    vmem = pl.BlockSpec(memory_space=pltpu.VMEM)
    return pl.pallas_call(
        kernel,
        out_shape=shapes,
        in_specs=[spec for _, spec in operands],
        out_specs=[vmem] * len(shapes),
        compiler_params=pltpu.CompilerParams(vmem_limit_bytes=10 * 2**20),
        cost_estimate=pl.CostEstimate(
            flops=int(microseconds * 1e9), bytes_accessed=2**20, transcendentals=0
        ),
    )(*[array for array, _ in operands])


def reduced(parts, *first):
    (total,) = call(total_kernel, [parts.shape[1:]], 1, whole(along_ring(parts)))
    across = [(r, r ^ 1) for r in range(lax.axis_size("row"))]
    other = lax.ppermute(total, "row", across)
    (spread,) = call(spread_kernel, [parts.shape], 1, whole(total), whole(other), *first)
    return along_ring(spread)


def shards(thickness, pairing):
    cells, width = thickness.shape
    half = width // 2
    slots = lax.axis_size("col")
    position = lax.axis_index("col")
    place = scalar(jnp.full((1,), position, jnp.int32))
    floor_value = math.sqrt(float(cells * lax.axis_size("row")))
    orders = [(whole(pairing[s]), whole(pairing[s].T)) for s in range(3)]
    block = whole(thickness)
    peers = lax.axis_size("row") // 2
    chunk = width // peers
    inside, outside = chip_swap(thickness), outer_swap(thickness)
    far_before, far_after = shifted(thickness, "col", 2), shifted(thickness, "col", -2)
    (own,) = call(own_gram_kernel, [(peers, chunk, width)], 1, block)
    own = reduced(own)
    ahead, before, after = call(
        functools.partial(ahead_kernel, slots),
        [(peers, 2 * chunk, width), (cells, width), (cells, width)],
        2,
        place,
        whole(outside),
        whole(inside),
        whole(far_after),
        whole(far_before),
    )
    shape = (2 * width + half + 8, half)
    inside, outside, data, pair = call(
        first_kernel,
        [shape, shape, (cells, width), (half, half)],
        6,
        place,
        whole(own),
        block,
        *orders[0],
    )
    sums = whole(reduced(ahead, after_it(inside)))
    outside, inside = outer_swap(outside), chip_swap(inside)
    inside, outside = call(
        second_kernel,
        [shape] * 2,
        8,
        place,
        whole(inside),
        whole(outside),
        sums,
        *orders[1],
    )
    outside, inside = outer_swap(outside), chip_swap(inside)
    inside, outside = call(
        functools.partial(third_kernel, floor_value),
        [(cells, half)] * 2,
        8,
        place,
        whole(outside),
        whole(inside),
        sums,
        whole(data),
        whole(pair),
        whole(before),
        whole(after),
        *orders[2],
    )
    outside, inside = outer_swap(outside), chip_swap(inside)
    even = lax.rem(position, 2) == 0
    return jnp.concatenate(in_order(even, inside, outside), axis=1)


def solution(mesh):
    placed = (P("row", "col"), P())
    return jax.shard_map(
        shards, mesh=mesh, in_specs=placed, out_specs=P("row", "col"), check_vma=False
    )
```
